256 devices in a mesh: tm: 64 (over y, z, core), lat: 4 (over x).
Axes of the slice: x: 4, y: 4, z: 8, core: 2. Of those that a mesh axis runs over, the one named last changes fastest.
Arguments:
- traj: float32 [64, 83, 24, 192], P('tm', None, 'lat'), may hold values from -6 to 6
- noise: float32 [64, 83, 24, 192], P('tm', None, 'lat'), may hold values from -6 to 6
- step_index: int32 [64], P('tm'), may hold values from 0 to 999
- embed_weight: bfloat16 [83, 512], replicated, may hold values from -0.625 to 0.625
- time_weight: float32 [512, 512], replicated, may hold values from -0.25 to 0.25
- dw_weight: float32 [512, 25], replicated, may hold values from -1.25 to 1.25
- ln_gain: float32 [512], replicated, may hold values from 0.5 to 1.5
- up_weight: bfloat16 [512, 1024], replicated, may hold values from -0.25 to 0.25
- down_weight: bfloat16 [1024, 512], replicated, may hold values from -0.1875 to 0.1875
- out_weight: bfloat16 [512, 83], replicated, may hold values from -0.25 to 0.25
Outputs:
- trajectory: float32 [64, 83, 24, 192], P('tm', None, 'lat')
The draws below stay inside these ranges and needn't reach their ends.
All inputs are finite; a program needn't handle non-finite values.
Results may differ from the reference program's by a relative error of at most 0.0025.
Values may be sent and summed in bfloat16 or wider, within the bound.
A program may use at most 128 MiB of HBM per device.

```python
import math
import jax
import jax.numpy as jnp
from jax import lax

D = 512
FF = 1024
CH = 83
LON = 192
ITERS = 2
LEVELS = 1000
TIMES = 64
NLAT = 24


def place_ends(drawn, rng, least, high):
    longest = drawn.shape.index(max(drawn.shape))
    spots = []
    for shift in (0, 1):
        where = [jax.random.randint(jax.random.fold_in(rng, axis), (), 0, length) for axis, length in enumerate(drawn.shape)]
        where[longest] = (where[longest] + shift) % drawn.shape[longest]
        spots.append(tuple(where))
    return drawn.at[spots[0]].set(least).at[spots[1]].set(high)


def block_scale(own_key, dims, shards, smallest, high):
    level, own = 1.0, jax.random.fold_in(own_key, 6)
    for axis_at, shards_of in shards:
        draws = jnp.exp(jax.random.uniform(jax.random.fold_in(own, axis_at), (shards_of,), jnp.float32, smallest / len(shards), high / len(shards)))
        level = level * jnp.repeat(draws, dims[axis_at] // shards_of).reshape([-1 if axis == axis_at else 1 for axis in range(len(dims))])
    return level


def bell_draw(rng, dims, spread, most, cuts=(), held_as=jnp.bfloat16):
    values = spread * jax.random.normal(rng, dims, jnp.float32)
    if cuts:
        values = values * block_scale(rng, dims, cuts, -0.22, 0.18)
    return jnp.clip(values, -most, most).astype(held_as)


def setup_inputs(seed: int = 0) -> dict:
    streams_of = jax.random.split(jax.random.key(seed), 11)
    return {
        "traj": bell_draw(streams_of[0], (TIMES, CH, NLAT, LON), 1.0, 6.0, ((0, 64), (2, 4)), jnp.float32),
        "noise": bell_draw(streams_of[1], (TIMES, CH, NLAT, LON), 1.0, 6.0, ((0, 64), (2, 4)), jnp.float32),
        "step_index": place_ends(jax.random.randint(streams_of[2], (TIMES,), 0, LEVELS), jax.random.fold_in(streams_of[2], 1), 0, LEVELS - 1).astype(jnp.int32),
        "embed_weight": bell_draw(streams_of[3], (CH, D), CH ** -0.5, 0.625),
        "time_weight": bell_draw(streams_of[4], (D, D), D ** -0.5, 0.25, (), jnp.float32),
        "dw_weight": bell_draw(streams_of[5], (D, 25), 25 ** -0.5, 1.25, (), jnp.float32),
        "ln_gain": jnp.clip(1.0 + 0.1 * jax.random.normal(streams_of[6], (D,), jnp.float32), 0.5, 1.5),
        "up_weight": bell_draw(streams_of[7], (D, FF), D ** -0.5, 0.25),
        "down_weight": bell_draw(streams_of[8], (FF, D), FF ** -0.5, 0.1875),
        "out_weight": bell_draw(streams_of[9], (D, CH), D ** -0.5, 0.25),
    }


def noise_levels(step_index):
    log_ratio = math.log(0.1) / (LEVELS - 1)
    return 2.0 * jnp.exp(step_index.astype(jnp.float32) * log_ratio)

def conditions(noise_level, time_weight):
    half_width = time_weight.shape[0] // 2
    frequency = jnp.exp(jnp.arange(half_width, dtype=jnp.float32) * (-math.log(100.0) / half_width))
    angles = jnp.log(noise_level)[:, None] * frequency[None, :]
    features = jnp.concatenate([jnp.cos(angles), jnp.sin(angles)], axis=1)
    return jax.nn.silu(jnp.dot(features, time_weight, precision=lax.Precision.HIGHEST))

def depthwise_taps(lat_padded, dw_weight):
    lat_rows = lat_padded.shape[1] - 4
    widened = lat_padded.astype(jnp.float32)
    lon_cols = widened.shape[2]
    widened = jnp.concatenate([widened[:, :, -2:], widened, widened[:, :, :2]], axis=2)
    summed = jnp.zeros((widened.shape[0], lat_rows, lon_cols), jnp.float32)
    for row_tap in range(5):
        for col_tap in range(5):
            summed = summed + dw_weight[:, row_tap * 5 + col_tap][:, None, None] * widened[:, row_tap:row_tap + lat_rows, col_tap:col_tap + lon_cols]
    return summed

def denoise(current, condition, embed_weight, dw_weight, ln_gain, up_weight, down_weight, out_weight):
    channels, lat_rows, lon_cols = current.shape
    as_rows = current.astype(jnp.bfloat16).reshape(channels, lat_rows * lon_cols)
    embedded = jnp.dot(embed_weight.T, as_rows, preferred_element_type=jnp.float32)
    activation = (embedded + condition[:, None]).astype(jnp.bfloat16)
    width = activation.shape[0]
    padded = jnp.pad(activation.reshape(width, lat_rows, lon_cols), ((0, 0), (2, 2), (0, 0)))
    convolved = depthwise_taps(padded, dw_weight).reshape(width, lat_rows * lon_cols)
    average = lax.optimization_barrier(jnp.mean(convolved, axis=0))
    centred = convolved - average[None, :]
    variance = lax.optimization_barrier(jnp.mean(centred * centred, axis=0))
    normed = (centred * lax.rsqrt(variance + 1e-06)[None, :] * ln_gain[:, None]).astype(jnp.bfloat16)
    hidden = jax.nn.gelu(jnp.dot(up_weight.T, normed, preferred_element_type=jnp.float32), approximate=True).astype(jnp.bfloat16)
    block_out = (activation.astype(jnp.float32) + jnp.dot(down_weight.T, hidden, preferred_element_type=jnp.float32)).astype(jnp.bfloat16)
    return jnp.dot(out_weight.T, block_out, preferred_element_type=jnp.float32).reshape(channels, lat_rows, lon_cols)

def reference(traj, noise, step_index, embed_weight, time_weight, dw_weight, ln_gain, up_weight, down_weight, out_weight):
    noise_level = noise_levels(step_index)
    condition = conditions(noise_level, time_weight)
    root = traj[0]
    current = traj
    for picard_step in range(ITERS):

        def one_time(pieces):
            state_now, cond_now, level_now, noise_now = pieces
            drift_term = denoise(state_now, cond_now, embed_weight, dw_weight, ln_gain, up_weight, down_weight, out_weight)
            return 0.125 * level_now * drift_term + 0.125 * jnp.sqrt(level_now) * noise_now
        increment = lax.map(one_time, (current, condition, noise_level, noise))
        earlier = jnp.cumsum(increment, axis=0) - increment
        current = root[None] + earlier
    return current
```

```python
import functools
import math

import jax
import jax.numpy as jnp
from jax import lax
from jax.experimental import pallas as pl
from jax.experimental.pallas import tpu as pltpu
from jax.sharding import PartitionSpec as P

MESH = pl.DeviceIdType.MESH
BF, F32 = jnp.bfloat16, jnp.float32
ITERS = 2
LEVELS = 1000
NCH, NROW, NLON = 83, 6, 192
SEG, COL = 8, 24
NT = 64
CHUNKS, TILES = 3, 18
OWNERS = CHUNKS * TILES
RET = (BF, F32)
D, FF = 512, 1024


def to_tiles(ref, lead, value):
    for lane in range(3):
        for group in range(6):
            ref[lead + (lane * 6 + group,)] = value[group * 16 : group * 16 + 16, lane * 128 : lane * 128 + 128]


def from_tiles(ref, lead):
    lanes = []
    for lane in range(3):
        lanes.append(jnp.concatenate([ref[lead + (lane * 6 + group,)].astype(F32) for group in range(6)], axis=0))
    return jnp.concatenate(lanes, axis=1)


def kernel(
    traj, noise, step, emb, timew, dw, gain, up_h, down_h, outw, out,
    up, down, act, wb, conv, vt, dt, nz, condb,
    ob, inb, retb0, retb1, st, stf, halo, rsrc, rbuf,
    wsem, osend, isem, rsend, stsem, hsend, hrecv, rootsend, rootrecv,
):
    t, l = lax.axis_index("tm"), lax.axis_index("lat")

    cup = pltpu.make_async_copy(up_h, up, wsem.at[0])
    cdown = pltpu.make_async_copy(down_h, down, wsem.at[1])
    cup.start()
    cdown.start()

    barrier = pltpu.get_barrier_semaphore()

    def greet(k, _):
        pl.semaphore_signal(barrier, inc=1, device_id={"tm": lax.rem(t + k, NT)}, device_id_type=MESH)
        return 0

    lax.fori_loop(1, NT, greet, 0)

    for shift in (1, 3):
        pl.semaphore_signal(barrier, inc=1, device_id={"lat": lax.rem(l + shift, 4)}, device_id_type=MESH)

    pad = jnp.zeros((96 - NCH, 384), F32)
    for b in range(CHUNKS):
        pair = jnp.concatenate([traj[0, :, 2 * b, :], traj[0, :, 2 * b + 1, :]], axis=1)
        dt[0:NCH, :] = pair
        dt[NCH:96, :] = pad
        whole = dt[0:96, :]
        to_tiles(rsrc.at[b], (), whole)
        to_tiles(st, (0, b), whole.astype(BF))
        nz[b, 0:NCH, :] = jnp.concatenate([noise[0, :, 2 * b, :], noise[0, :, 2 * b + 1, :]], axis=1)
        nz[b, NCH:96, :] = pad

    stepf = jnp.full((8, 512), step[0].astype(F32), F32)
    level = 2.0 * jnp.exp(stepf * (math.log(0.1) / (LEVELS - 1)))
    j = lax.broadcasted_iota(jnp.int32, (8, 512), 1)
    jj = jnp.where(j < 256, j, j - 256).astype(F32)
    frequency = jnp.exp(jj * (-math.log(100.0) / 256))
    angles = jnp.log(level) * frequency
    features = jnp.where(j < 256, jnp.cos(angles), jnp.sin(angles))
    cond = jnp.dot(features, timew[...], precision=lax.Precision.HIGHEST, preferred_element_type=F32)
    condb[...] = cond * (1.0 / (1.0 + jnp.exp(-cond)))
    drift_scale = 0.125 * level[0:1, 0:384]
    noise_scale = 0.125 * jnp.sqrt(level[0:1, 0:384])

    taps = jnp.transpose(dw[...])
    for k in range(25):
        wb[k] = jnp.broadcast_to(taps[k : k + 1, :], (8, D))

    pl.semaphore_wait(barrier, NT + 1)

    def halo_up(it):
        return pltpu.make_async_remote_copy(
            src_ref=st.at[it, 0], dst_ref=halo.at[it, 1], send_sem=hsend.at[it, 0], recv_sem=hrecv.at[it, 1],
            device_id={"lat": l - 1}, device_id_type=MESH)

    def halo_down(it):
        return pltpu.make_async_remote_copy(
            src_ref=st.at[it, 2], dst_ref=halo.at[it, 0], send_sem=hsend.at[it, 1], recv_sem=hrecv.at[it, 0],
            device_id={"lat": l + 1}, device_id_type=MESH)

    def start_up(it):
        @pl.when(l > 0)
        def _():
            halo_up(it).start()

    def start_down(it):
        @pl.when(l < 3)
        def _():
            halo_down(it).start()

    start_up(0)
    start_down(0)

    def root_copy(k):
        return pltpu.make_async_remote_copy(
            src_ref=rsrc.at[k % 3, k // 3], dst_ref=rbuf, send_sem=rootsend, recv_sem=rootrecv,
            device_id={"tm": k}, device_id_type=MESH)

    @pl.when(t == 0)
    def _():
        pltpu.make_async_copy(rsrc.at[0, 0], rbuf, rootrecv).start()

        def one(k, _):
            root_copy(k).start()
            return 0

        lax.fori_loop(1, OWNERS, one, 0)

    def embed(read, row0):
        vt[:, 0:96] = jnp.transpose(read)

        for rr in range(2):
            cols = [vt[pl.ds(rr * NLON + c, SEG, stride=COL), :] for c in range(COL)]
            lhs = jnp.concatenate(cols, axis=0)[:, 0:NCH].astype(BF)
            value = jnp.dot(lhs, emb[...], preferred_element_type=F32)
            value = value.reshape(COL, SEG, D) + condb[...][None]
            value = value.astype(BF).astype(F32)
            act[row0 + rr, 2 : 2 + COL] = value
            for c in range(2):
                act[row0 + rr, c] = pltpu.roll(value[COL - 2 + c], 1, 0)
                act[row0 + rr, COL + 2 + c] = pltpu.roll(value[c], SEG - 1, 0)

    def zero_rows(row0):
        act[pl.ds(row0, 2)] = jnp.zeros((2, COL + 4, SEG, D), F32)

    def convolve(b):
        for g in range(4):
            lanes = slice(g * 128, g * 128 + 128)

            def block(cb, _):
                c0 = cb * 4
                acc = [[None] * 4 for _ in range(2)]
                for ri in range(6):
                    xs = [act[2 * b + ri, c0 + ci, :, lanes] for ci in range(8)]
                    for rr in range(2):
                        tap = ri - rr
                        if not 0 <= tap < 5:
                            continue
                        for cc in range(4):
                            for tj in range(5):
                                term = wb[tap * 5 + tj, :, lanes] * xs[cc + tj]
                                acc[rr][cc] = term if acc[rr][cc] is None else acc[rr][cc] + term
                for rr in range(2):
                    for cc in range(4):
                        conv[rr, c0 + cc, :, lanes] = acc[rr][cc]
                return 0

            lax.fori_loop(0, 6, block, 0)

    def mlp(b):
        for rr in range(2):
            x = conv[rr].reshape(NLON, D)
            mean = jnp.mean(x, axis=1, keepdims=True)
            x = x - mean
            var = jnp.mean(x * x, axis=1, keepdims=True)
            normed = (x * lax.rsqrt(var + 1e-6) * gain[...]).astype(BF)
            h = jnp.dot(normed, up[...], preferred_element_type=F32)
            inner = 0.7978845608028654 * (h + 0.044715 * (h * h * h))
            hidden = (0.5 * h * (1.0 + jnp.tanh(inner))).astype(BF)
            y = jnp.dot(hidden, down[...], preferred_element_type=F32)
            y = (act[2 + 2 * b + rr, 2 : 2 + COL].reshape(NLON, D) + y).astype(BF)
            drift = jnp.dot(y, outw[...], preferred_element_type=F32)
            for c in range(COL):
                vt[pl.ds(rr * NLON + c, SEG, stride=COL), 0:NCH] = drift[c * SEG : c * SEG + SEG, :]
        dT = jnp.transpose(vt[...])[0:96, :]
        return drift_scale * dT + noise_scale * nz[b]

    def send_chunk(it, b):
        def one(k, _):
            owner = 3 * k + b

            @pl.when(owner == t)
            def _():
                pltpu.make_async_copy(ob.at[it, b, k], inb.at[it, t], isem.at[it]).start()

            @pl.when(owner != t)
            def _():
                pltpu.make_async_remote_copy(
                    src_ref=ob.at[it, b, k], dst_ref=inb.at[it, t], send_sem=osend.at[it, b], recv_sem=isem.at[it],
                    device_id={"tm": owner}, device_id_type=MESH).start()

            return 0

        lax.fori_loop(0, TILES, one, 0)

    mine_b, mine_k = lax.rem(t, 3), t // 3

    def scan(it):
        retb = (retb0, retb1)[it]
        dst = (st.at[1], stf)[it]

        @pl.when(t < OWNERS)
        def _():
            if it == 0:
                pltpu.make_async_copy(rbuf, rbuf, rootrecv).wait()
            pltpu.make_async_copy(inb.at[it], inb.at[it], isem.at[it]).wait()

            def one(s, acc):
                retb[s] = acc.astype(retb.dtype)

                @pl.when(s == t)
                def _():
                    pltpu.make_async_copy(retb.at[s], dst.at[mine_b, mine_k], stsem.at[it, mine_b]).start()

                @pl.when(s != t)
                def _():
                    pltpu.make_async_remote_copy(
                        src_ref=retb.at[s], dst_ref=dst.at[mine_b, mine_k], send_sem=rsend.at[it],
                        recv_sem=stsem.at[it, mine_b], device_id={"tm": s}, device_id_type=MESH).start()

                return acc + inb[it, s].astype(F32)

            lax.fori_loop(0, NT, one, rbuf[...])

    def wait_chunk(it, b):
        dst = (st.at[1], stf)[it]
        pltpu.make_async_copy(dst.at[b], dst.at[b], stsem.at[it, b]).wait()

    cup.wait()
    cdown.wait()
    vt[...] = jnp.zeros(vt.shape, F32)
    for it in range(ITERS):
        if it == 1:
            wait_chunk(0, 0)
            start_up(1)
            wait_chunk(0, 2)
            start_down(1)
            wait_chunk(0, 1)
        for b in range(CHUNKS):
            embed(from_tiles(st, (it, b)), 2 + 2 * b)
        for b in (1, 0, 2):
            if b == 0:
                @pl.when(l > 0)
                def _():
                    halo_up(it).wait_send()
                    pltpu.make_async_copy(halo.at[it, 0], halo.at[it, 0], hrecv.at[it, 0]).wait()
                    embed(from_tiles(halo, (it, 0)), 0)

                @pl.when(l == 0)
                def _():
                    zero_rows(0)
            if b == 2:
                @pl.when(l < 3)
                def _():
                    halo_down(it).wait_send()
                    pltpu.make_async_copy(halo.at[it, 1], halo.at[it, 1], hrecv.at[it, 1]).wait()
                    embed(from_tiles(halo, (it, 1)), 8)

                @pl.when(l == 3)
                def _():
                    zero_rows(8)
            convolve(b)
            to_tiles(ob, (it, b), mlp(b).astype(BF))
            send_chunk(it, b)
        scan(it)

    for b in (1, 0, 2):
        wait_chunk(1, b)
        value = from_tiles(stf, (b,))[0:NCH, :]
        out[0, :, 2 * b, :] = value[:, 0:NLON]
        out[0, :, 2 * b + 1, :] = value[:, NLON : 2 * NLON]

    def drain(ref, sem):
        pltpu.make_async_copy(ref, ref, sem).wait()

    @pl.when(t == 0)
    def _():
        drain(rsrc.at[0], rootsend)
        drain(rsrc.at[1], rootsend)
        drain(rsrc.at[2, pl.ds(0, TILES - 1)], rootsend)

    for it in range(ITERS):
        for b in range(CHUNKS):
            own = jnp.logical_and(mine_b == b, t < OWNERS)

            @pl.when(own)
            def _():
                drain(ob.at[it, b, pl.ds(0, TILES - 1)], osend.at[it, b])

            @pl.when(jnp.logical_not(own))
            def _():
                drain(ob.at[it, b], osend.at[it, b])

        @pl.when(t < OWNERS)
        def _():
            retb = (retb0, retb1)[it]
            drain(retb.at[pl.ds(0, NT - 1)], rsend.at[it])


def shards(traj, noise, step_index, emb, timew, dw, gain, up, down, outw):
    vm = pl.BlockSpec(memory_space=pltpu.VMEM)
    anyspace = pl.BlockSpec(memory_space=pl.ANY)
    dma = pltpu.SemaphoreType.DMA
    return pl.pallas_call(
        kernel,
        out_shape=jax.ShapeDtypeStruct((1, NCH, NROW, NLON), F32),
        in_specs=[vm, vm, pl.BlockSpec(memory_space=pltpu.SMEM), vm, vm, vm, vm, anyspace, anyspace, vm],
        out_specs=vm,
        scratch_shapes=[
            pltpu.VMEM((D, FF), BF),
            pltpu.VMEM((FF, D), BF),
            pltpu.VMEM((10, COL + 4, SEG, D), F32),
            pltpu.VMEM((25, 8, D), F32),
            pltpu.VMEM((2, COL, SEG, D), F32),
            pltpu.VMEM((384, 128), F32),
            pltpu.VMEM((96, 384), F32),
            pltpu.VMEM((CHUNKS, 96, 384), F32),
            pltpu.VMEM((8, D), F32),
            pltpu.VMEM((ITERS, CHUNKS, TILES, 16, 128), BF),
            pltpu.VMEM((ITERS, NT, 16, 128), BF),
            pltpu.VMEM((NT, 16, 128), RET[0]),
            pltpu.VMEM((NT, 16, 128), RET[1]),
            pltpu.VMEM((ITERS, CHUNKS, TILES, 16, 128), BF),
            pltpu.VMEM((CHUNKS, TILES, 16, 128), RET[1]),
            pltpu.VMEM((ITERS, 2, TILES, 16, 128), BF),
            pltpu.VMEM((CHUNKS, TILES, 16, 128), F32),
            pltpu.VMEM((16, 128), F32),
            dma((2,)),
            dma((ITERS, CHUNKS)),
            dma((ITERS,)),
            dma((ITERS,)),
            dma((ITERS, CHUNKS)),
            dma((ITERS, 2)),
            dma((ITERS, 2)),
            dma,
            dma,
        ],
        compiler_params=pltpu.CompilerParams(
            collective_id=0, has_side_effects=True, vmem_limit_bytes=56 * 2**20
        ),
    )(traj, noise, step_index, emb, timew, dw, gain.reshape(1, D), up, down, outw)


def solution(mesh):
    in_specs = (
        P("tm", None, "lat", None),
        P("tm", None, "lat", None),
        P("tm"),
        P(), P(), P(), P(), P(), P(), P(),
    )
    out_specs = P("tm", None, "lat", None)
    return jax.shard_map(shards, mesh=mesh, in_specs=in_specs, out_specs=out_specs, check_vma=False)
```

```python
import functools
import math

import jax
import jax.numpy as jnp
from jax import lax
from jax.experimental import pallas as pl
from jax.experimental.pallas import tpu as pltpu
from jax.sharding import PartitionSpec as P

MESH = pl.DeviceIdType.MESH
BF, F32 = jnp.bfloat16, jnp.float32
ITERS = 2
LEVELS = 1000
NCH, NROW, NLON = 83, 6, 192
SEG, COL = 8, 24
NT = 64
CHUNKS, TILES = 3, 18
OWNERS = CHUNKS * TILES
RET = (BF, F32)
D, FF = 512, 1024


def to_tiles(ref, lead, value):
    for lane in range(3):
        for group in range(6):
            ref[lead + (lane * 6 + group,)] = value[group * 16 : group * 16 + 16, lane * 128 : lane * 128 + 128]


def from_tiles(ref, lead):
    lanes = []
    for lane in range(3):
        lanes.append(jnp.concatenate([ref[lead + (lane * 6 + group,)].astype(F32) for group in range(6)], axis=0))
    return jnp.concatenate(lanes, axis=1)


def kernel(
    traj, noise, step, emb, timew_h, taps, gain, up_h, down_h, outw, out,
    up, down, timew, tin, nin, tout, act, wb, conv, vt, dt, nz, condb,
    ob, inb, retb0, retb1, st, stf, halo, rsrc, rbuf,
    wsem, iosem, osend, isem, rsend, stsem, hsend, hrecv, rootsend, rootrecv,
):
    t, l = lax.axis_index("tm"), lax.axis_index("lat")

    def traj_in(r):
        return pltpu.make_async_copy(traj.at[:, r, 0, :], tin.at[r], iosem.at[0, r])

    def noise_in(r):
        return pltpu.make_async_copy(noise.at[:, r, 0, :], nin.at[r], iosem.at[1, r])

    def state_out(r):
        return pltpu.make_async_copy(tout.at[r], out.at[:, r, 0, :], iosem.at[2, r])

    for r in range(NROW):
        traj_in(r).start()
    ctime = pltpu.make_async_copy(timew_h, timew, wsem.at[2])
    ctime.start()
    for r in range(NROW):
        noise_in(r).start()
    cup = pltpu.make_async_copy(up_h, up, wsem.at[0])
    cdown = pltpu.make_async_copy(down_h, down, wsem.at[1])
    cup.start()
    cdown.start()

    barrier = pltpu.get_barrier_semaphore()

    def greet(k, _):
        pl.semaphore_signal(barrier, inc=1, device_id={"tm": lax.rem(t + k, NT)}, device_id_type=MESH)
        return 0

    lax.fori_loop(1, NT, greet, 0)

    for shift in (1, 3):
        pl.semaphore_signal(barrier, inc=1, device_id={"lat": lax.rem(l + shift, 4)}, device_id_type=MESH)

    for r in range(NROW):
        traj_in(r).wait()
    pad = jnp.zeros((96 - NCH, 384), F32)
    for b in range(CHUNKS):
        pair = jnp.concatenate([tin[2 * b], tin[2 * b + 1]], axis=1)
        dt[0:NCH, :] = pair
        dt[NCH:96, :] = pad
        whole = dt[0:96, :]
        to_tiles(rsrc.at[b], (), whole)
        to_tiles(st, (0, b), whole.astype(BF))

    stepf = jnp.full((8, 512), step[0].astype(F32), F32)
    level = 2.0 * jnp.exp(stepf * (math.log(0.1) / (LEVELS - 1)))
    j = lax.broadcasted_iota(jnp.int32, (8, 512), 1)
    jj = jnp.where(j < 256, j, j - 256).astype(F32)
    frequency = jnp.exp(jj * (-math.log(100.0) / 256))
    angles = jnp.log(level) * frequency
    features = jnp.where(j < 256, jnp.cos(angles), jnp.sin(angles))
    ctime.wait()
    cond = jnp.dot(features, timew[...], precision=lax.Precision.HIGHEST, preferred_element_type=F32)
    condb[...] = cond * (1.0 / (1.0 + jnp.exp(-cond)))
    drift_scale = 0.125 * level[0:1, 0:384]
    noise_scale = 0.125 * jnp.sqrt(level[0:1, 0:384])

    for k in range(25):
        wb[k] = jnp.broadcast_to(taps[k : k + 1, :], (8, D))

    def halo_up(it):
        return pltpu.make_async_remote_copy(
            src_ref=st.at[it, 0], dst_ref=halo.at[it, 1], send_sem=hsend.at[it, 0], recv_sem=hrecv.at[it, 1],
            device_id={"lat": l - 1}, device_id_type=MESH)

    def halo_down(it):
        return pltpu.make_async_remote_copy(
            src_ref=st.at[it, 2], dst_ref=halo.at[it, 0], send_sem=hsend.at[it, 1], recv_sem=hrecv.at[it, 0],
            device_id={"lat": l + 1}, device_id_type=MESH)

    def start_up(it):
        @pl.when(l > 0)
        def _():
            halo_up(it).start()

    def start_down(it):
        @pl.when(l < 3)
        def _():
            halo_down(it).start()

    def root_copy(k):
        return pltpu.make_async_remote_copy(
            src_ref=rsrc.at[k % 3, k // 3], dst_ref=rbuf, send_sem=rootsend, recv_sem=rootrecv,
            device_id={"tm": k}, device_id_type=MESH)

    def meet():
        pl.semaphore_wait(barrier, NT + 1)
        start_up(0)
        start_down(0)

        @pl.when(t == 0)
        def _():
            pltpu.make_async_copy(rsrc.at[0, 0], rbuf, rootrecv).start()

            def one(k, _):
                root_copy(k).start()
                return 0

            lax.fori_loop(1, OWNERS, one, 0)

    def embed(read, row0):
        vt[:, 0:96] = jnp.transpose(read)

        for rr in range(2):
            cols = [vt[pl.ds(rr * NLON + c, SEG, stride=COL), :] for c in range(COL)]
            lhs = jnp.concatenate(cols, axis=0)[:, 0:NCH].astype(BF)
            value = jnp.dot(lhs, emb[...], preferred_element_type=F32)
            value = value.reshape(COL, SEG, D) + condb[...][None]
            value = value.astype(BF).astype(F32)
            act[row0 + rr, 2 : 2 + COL] = value
            for c in range(2):
                act[row0 + rr, c] = pltpu.roll(value[COL - 2 + c], 1, 0)
                act[row0 + rr, COL + 2 + c] = pltpu.roll(value[c], SEG - 1, 0)

    def zero_rows(row0):
        act[pl.ds(row0, 2)] = jnp.zeros((2, COL + 4, SEG, D), F32)

    def convolve(b):
        for g in range(4):
            lanes = slice(g * 128, g * 128 + 128)
            weight = [wb[k, :, lanes] for k in range(25)]

            def block(cb, _):
                c0 = cb * 2
                acc = [[None] * 2 for _ in range(2)]
                for ri in range(6):
                    xs = [act[2 * b + ri, c0 + ci, :, lanes] for ci in range(6)]
                    for rr in range(2):
                        tap = ri - rr
                        if not 0 <= tap < 5:
                            continue
                        for cc in range(2):
                            for tj in range(5):
                                term = weight[tap * 5 + tj] * xs[cc + tj]
                                acc[rr][cc] = term if acc[rr][cc] is None else acc[rr][cc] + term
                for rr in range(2):
                    for cc in range(2):
                        conv[rr, c0 + cc, :, lanes] = acc[rr][cc]
                return 0

            lax.fori_loop(0, COL // 2, block, 0)

    def mlp(b):
        for rr in range(2):
            x = conv[rr].reshape(NLON, D)
            mean = jnp.mean(x, axis=1, keepdims=True)
            x = x - mean
            var = jnp.mean(x * x, axis=1, keepdims=True)
            normed = (x * lax.rsqrt(var + 1e-6) * gain[...]).astype(BF)
            h = jnp.dot(normed, up[...], preferred_element_type=F32)
            inner = 0.7978845608028654 * (h + 0.044715 * (h * h * h))
            hidden = (0.5 * h * (1.0 + jnp.tanh(inner))).astype(BF)
            y = jnp.dot(hidden, down[...], preferred_element_type=F32)
            y = (act[2 + 2 * b + rr, 2 : 2 + COL].reshape(NLON, D) + y).astype(BF)
            drift = lax.dot_general(y, outw[...], (((1,), (1,)), ((), ())), preferred_element_type=F32)
            for c in range(COL):
                vt[pl.ds(rr * NLON + c, SEG, stride=COL), 0:NCH] = drift[c * SEG : c * SEG + SEG, :]
        dT = jnp.transpose(vt[...])[0:96, :]
        return drift_scale * dT + noise_scale * nz[b]

    def send_chunk(it, b):
        def one(k, _):
            owner = 3 * k + b

            @pl.when(owner == t)
            def _():
                pltpu.make_async_copy(ob.at[it, b, k], inb.at[it, t], isem.at[it]).start()

            @pl.when(owner != t)
            def _():
                pltpu.make_async_remote_copy(
                    src_ref=ob.at[it, b, k], dst_ref=inb.at[it, t], send_sem=osend.at[it, b], recv_sem=isem.at[it],
                    device_id={"tm": owner}, device_id_type=MESH).start()

            return 0

        lax.fori_loop(0, TILES, one, 0)

    mine_b, mine_k = lax.rem(t, 3), t // 3

    def scan(it):
        retb = (retb0, retb1)[it]
        dst = (st.at[1], stf)[it]

        @pl.when(t < OWNERS)
        def _():
            if it == 0:
                pltpu.make_async_copy(rbuf, rbuf, rootrecv).wait()
            pltpu.make_async_copy(inb.at[it], inb.at[it], isem.at[it]).wait()

            def one(s, acc):
                retb[s] = acc.astype(retb.dtype)

                @pl.when(s == t)
                def _():
                    pltpu.make_async_copy(retb.at[s], dst.at[mine_b, mine_k], stsem.at[it, mine_b]).start()

                @pl.when(s != t)
                def _():
                    pltpu.make_async_remote_copy(
                        src_ref=retb.at[s], dst_ref=dst.at[mine_b, mine_k], send_sem=rsend.at[it],
                        recv_sem=stsem.at[it, mine_b], device_id={"tm": s}, device_id_type=MESH).start()

                return acc + inb[it, s].astype(F32)

            lax.fori_loop(0, NT, one, rbuf[...])

    def wait_chunk(it, b):
        dst = (st.at[1], stf)[it]
        pltpu.make_async_copy(dst.at[b], dst.at[b], stsem.at[it, b]).wait()

    vt[...] = jnp.zeros(vt.shape, F32)
    for it in range(ITERS):
        if it == 1:
            wait_chunk(0, 0)
            start_up(1)
            wait_chunk(0, 2)
            start_down(1)
            wait_chunk(0, 1)
        for b in range(CHUNKS):
            embed(from_tiles(st, (it, b)), 2 + 2 * b)
        for b in (1, 0, 2):
            if b == 0:
                @pl.when(l > 0)
                def _():
                    halo_up(it).wait_send()
                    pltpu.make_async_copy(halo.at[it, 0], halo.at[it, 0], hrecv.at[it, 0]).wait()
                    embed(from_tiles(halo, (it, 0)), 0)

                @pl.when(l == 0)
                def _():
                    zero_rows(0)
            if b == 2:
                @pl.when(l < 3)
                def _():
                    halo_down(it).wait_send()
                    pltpu.make_async_copy(halo.at[it, 1], halo.at[it, 1], hrecv.at[it, 1]).wait()
                    embed(from_tiles(halo, (it, 1)), 8)

                @pl.when(l == 3)
                def _():
                    zero_rows(8)
            convolve(b)
            if it == 0 and b == 1:
                meet()
                for r in range(NROW):
                    noise_in(r).wait()
                for bb in range(CHUNKS):
                    nz[bb, 0:NCH, :] = jnp.concatenate([nin[2 * bb], nin[2 * bb + 1]], axis=1)
                    nz[bb, NCH:96, :] = pad
                cup.wait()
                cdown.wait()
            to_tiles(ob, (it, b), mlp(b).astype(BF))
            send_chunk(it, b)
        scan(it)

    for b in (1, 0, 2):
        wait_chunk(1, b)
        value = from_tiles(stf, (b,))[0:NCH, :]
        for rr in range(2):
            tout[2 * b + rr] = value[:, rr * NLON : rr * NLON + NLON]
            state_out(2 * b + rr).start()

    def drain(ref, sem):
        pltpu.make_async_copy(ref, ref, sem).wait()

    @pl.when(t == 0)
    def _():
        drain(rsrc.at[0], rootsend)
        drain(rsrc.at[1], rootsend)
        drain(rsrc.at[2, pl.ds(0, TILES - 1)], rootsend)

    for r in range(NROW):
        state_out(r).wait()

    for it in range(ITERS):
        for b in range(CHUNKS):
            own = jnp.logical_and(mine_b == b, t < OWNERS)

            @pl.when(own)
            def _():
                drain(ob.at[it, b, pl.ds(0, TILES - 1)], osend.at[it, b])

            @pl.when(jnp.logical_not(own))
            def _():
                drain(ob.at[it, b], osend.at[it, b])

        @pl.when(t < OWNERS)
        def _():
            retb = (retb0, retb1)[it]
            drain(retb.at[pl.ds(0, NT - 1)], rsend.at[it])


def shards(traj, noise, step_index, emb, timew, dw, gain, up, down, outw):
    vm = pl.BlockSpec(memory_space=pltpu.VMEM)
    anyspace = pl.BlockSpec(memory_space=pl.ANY)
    dma = pltpu.SemaphoreType.DMA
    result = pl.pallas_call(
        kernel,
        out_shape=jax.ShapeDtypeStruct((NCH, NROW, 1, NLON), F32),
        in_specs=[anyspace, anyspace, pl.BlockSpec(memory_space=pltpu.SMEM), vm, anyspace, vm, vm, anyspace, anyspace, vm],
        out_specs=anyspace,
        scratch_shapes=[
            pltpu.VMEM((D, FF), BF),
            pltpu.VMEM((FF, D), BF),
            pltpu.VMEM((D, D), F32),
            pltpu.VMEM((NROW, NCH, NLON), F32),
            pltpu.VMEM((NROW, NCH, NLON), F32),
            pltpu.VMEM((NROW, NCH, NLON), F32),
            pltpu.VMEM((10, COL + 4, SEG, D), F32),
            pltpu.VMEM((25, 8, D), F32),
            pltpu.VMEM((2, COL, SEG, D), F32),
            pltpu.VMEM((384, 128), F32),
            pltpu.VMEM((96, 384), F32),
            pltpu.VMEM((CHUNKS, 96, 384), F32),
            pltpu.VMEM((8, D), F32),
            pltpu.VMEM((ITERS, CHUNKS, TILES, 16, 128), BF),
            pltpu.VMEM((ITERS, NT, 16, 128), BF),
            pltpu.VMEM((NT, 16, 128), RET[0]),
            pltpu.VMEM((NT, 16, 128), RET[1]),
            pltpu.VMEM((ITERS, CHUNKS, TILES, 16, 128), BF),
            pltpu.VMEM((CHUNKS, TILES, 16, 128), RET[1]),
            pltpu.VMEM((ITERS, 2, TILES, 16, 128), BF),
            pltpu.VMEM((CHUNKS, TILES, 16, 128), F32),
            pltpu.VMEM((16, 128), F32),
            dma((3,)),
            dma((3, NROW)),
            dma((ITERS, CHUNKS)),
            dma((ITERS,)),
            dma((ITERS,)),
            dma((ITERS, CHUNKS)),
            dma((ITERS, 2)),
            dma((ITERS, 2)),
            dma,
            dma,
        ],
        compiler_params=pltpu.CompilerParams(
            collective_id=0, has_side_effects=True, vmem_limit_bytes=56 * 2**20
        ),
    )(
        traj.reshape(NCH, NROW, 1, NLON), noise.reshape(NCH, NROW, 1, NLON), step_index,
        emb, timew, dw.T, gain.reshape(1, D), up, down, outw.T,
    )
    return result.reshape(1, NCH, NROW, NLON)


def solution(mesh):
    in_specs = (
        P("tm", None, "lat", None),
        P("tm", None, "lat", None),
        P("tm"),
        P(), P(), P(), P(), P(), P(), P(),
    )
    out_specs = P("tm", None, "lat", None)
    return jax.shard_map(shards, mesh=mesh, in_specs=in_specs, out_specs=out_specs, check_vma=False)
```

```python
import functools
import math

import jax
import jax.numpy as jnp
from jax import lax
from jax.experimental import pallas as pl
from jax.experimental.pallas import tpu as pltpu
from jax.sharding import PartitionSpec as P

MESH = pl.DeviceIdType.MESH
BF, F32 = jnp.bfloat16, jnp.float32
ITERS = 2
LEVELS = 1000
NCH, NROW, NLON = 83, 6, 192
SEG, COL = 8, 24
NT = 64
CHUNKS, TILES = 3, 18
OWNERS = CHUNKS * TILES
RET = (BF, BF)
D, FF = 512, 1024


def to_tiles(ref, lead, value):
    for lane in range(3):
        for group in range(6):
            ref[lead + (lane * 6 + group,)] = value[group * 16 : group * 16 + 16, lane * 128 : lane * 128 + 128]


def from_tiles(ref, lead):
    lanes = []
    for lane in range(3):
        lanes.append(jnp.concatenate([ref[lead + (lane * 6 + group,)].astype(F32) for group in range(6)], axis=0))
    return jnp.concatenate(lanes, axis=1)


def kernel(
    traj, noise, step, emb, timew_h, taps, gain, up_h, down_h, outw, out,
    up, down, timew, tin, nin, tout, act, wb, conv, vt, dt, nz, condb,
    ob, inb, retb0, retb1, st, stf, halo, rsrc, rbuf,
    wsem, iosem, osend, isem, rsend, stsem, hsend, hrecv, rootsend, rootrecv,
):
    t, l = lax.axis_index("tm"), lax.axis_index("lat")
    y, z, core = t // 16, (t // 2) % 8, t % 2

    def others(do):
        def ring(i, _):
            half = (i + 1) // 2
            dz = jnp.where(i % 2 == 0, 4 + half, 4 - half)
            zz = lax.rem(z + dz, 8) * 2
            for dy in (2, 1, 3, 0):
                yy = lax.rem(y + dy, 4) * 16 + zz
                for dc in (0, 1):
                    do(yy + lax.rem(core + dc, 2))
            return 0

        lax.fori_loop(0, 7, ring, 0)
        for dy in (2, 1, 3, 0):
            for dc in (1, 0):
                if dy or dc:
                    do(lax.rem(y + dy, 4) * 16 + z * 2 + lax.rem(core + dc, 2))

    barrier = pltpu.get_barrier_semaphore()
    for shift in (1, 3):
        pl.semaphore_signal(barrier, inc=1, device_id={"lat": lax.rem(l + shift, 4)}, device_id_type=MESH)
    others(lambda s: pl.semaphore_signal(barrier, inc=1, device_id={"tm": s}, device_id_type=MESH))


    def traj_in(r):
        return pltpu.make_async_copy(traj.at[:, r, 0, :], tin.at[r], iosem.at[0, r])

    def noise_in(r):
        return pltpu.make_async_copy(noise.at[:, r, 0, :], nin.at[r], iosem.at[1, r])

    def state_out(r):
        return pltpu.make_async_copy(tout.at[r], out.at[:, r, 0, :], iosem.at[2, r])

    for r in range(NROW):
        traj_in(r).start()
    ctime = pltpu.make_async_copy(timew_h, timew, wsem.at[2])
    ctime.start()
    for r in range(NROW):
        noise_in(r).start()
    cup = pltpu.make_async_copy(up_h, up, wsem.at[0])
    cdown = pltpu.make_async_copy(down_h, down, wsem.at[1])
    cup.start()
    cdown.start()

    for r in range(NROW):
        traj_in(r).wait()
    pad = jnp.zeros((96 - NCH, 384), F32)
    for b in range(CHUNKS):
        pair = jnp.concatenate([tin[2 * b], tin[2 * b + 1]], axis=1)
        dt[0:NCH, :] = pair
        dt[NCH:96, :] = pad
        whole = dt[0:96, :]
        to_tiles(rsrc.at[b], (), whole)
        to_tiles(st, (0, b), whole.astype(BF))

    stepf = jnp.full((8, 512), step[0].astype(F32), F32)
    level = 2.0 * jnp.exp(stepf * (math.log(0.1) / (LEVELS - 1)))
    j = lax.broadcasted_iota(jnp.int32, (8, 512), 1)
    jj = jnp.where(j < 256, j, j - 256).astype(F32)
    frequency = jnp.exp(jj * (-math.log(100.0) / 256))
    angles = jnp.log(level) * frequency
    features = jnp.where(j < 256, jnp.cos(angles), jnp.sin(angles))
    ctime.wait()
    cond = jnp.dot(features, timew[...], precision=lax.Precision.HIGHEST, preferred_element_type=F32)
    condb[...] = cond * (1.0 / (1.0 + jnp.exp(-cond)))
    drift_scale = 0.125 * level[0:1, 0:384]
    noise_scale = 0.125 * jnp.sqrt(level[0:1, 0:384])

    for k in range(25):
        wb[k] = jnp.broadcast_to(taps[k : k + 1, :], (8, D))

    def halo_up(it):
        return pltpu.make_async_remote_copy(
            src_ref=st.at[it, 0], dst_ref=halo.at[it, 1], send_sem=hsend.at[it, 0], recv_sem=hrecv.at[it, 1],
            device_id={"lat": l - 1}, device_id_type=MESH)

    def halo_down(it):
        return pltpu.make_async_remote_copy(
            src_ref=st.at[it, 2], dst_ref=halo.at[it, 0], send_sem=hsend.at[it, 1], recv_sem=hrecv.at[it, 0],
            device_id={"lat": l + 1}, device_id_type=MESH)

    def start_up(it):
        @pl.when(l > 0)
        def _():
            halo_up(it).start()

    def start_down(it):
        @pl.when(l < 3)
        def _():
            halo_down(it).start()

    def root_copy(k):
        return pltpu.make_async_remote_copy(
            src_ref=rsrc.at[k % 3, k // 3], dst_ref=rbuf, send_sem=rootsend, recv_sem=rootrecv,
            device_id={"tm": k}, device_id_type=MESH)

    def meet():
        pl.semaphore_wait(barrier, NT + 1)
        start_up(0)
        start_down(0)

        @pl.when(t == 0)
        def _():
            pltpu.make_async_copy(rsrc.at[0, 0], rbuf, rootrecv).start()

            def one(k, _):
                root_copy(k).start()
                return 0

            lax.fori_loop(1, OWNERS, one, 0)

    def embed(read, row0):
        vt[:, 0:96] = jnp.transpose(read)

        for rr in range(2):
            cols = [vt[pl.ds(rr * NLON + c, SEG, stride=COL), :] for c in range(COL)]
            lhs = jnp.concatenate(cols, axis=0)[:, 0:NCH].astype(BF)
            value = jnp.dot(lhs, emb[...], preferred_element_type=F32)
            value = value.reshape(COL, SEG, D) + condb[...][None]
            value = value.astype(BF).astype(F32)
            act[row0 + rr, 2 : 2 + COL] = value
            for c in range(2):
                act[row0 + rr, c] = pltpu.roll(value[COL - 2 + c], 1, 0)
                act[row0 + rr, COL + 2 + c] = pltpu.roll(value[c], SEG - 1, 0)

    def zero_rows(row0):
        act[pl.ds(row0, 2)] = jnp.zeros((2, COL + 4, SEG, D), F32)

    def convolve(b):
        for g in range(4):
            lanes = slice(g * 128, g * 128 + 128)
            weight = [wb[k, :, lanes] for k in range(25)]

            def block(cb, _):
                c0 = cb * 2
                acc = [[None] * 2 for _ in range(2)]
                for ri in range(6):
                    xs = [act[2 * b + ri, c0 + ci, :, lanes] for ci in range(6)]
                    for rr in range(2):
                        tap = ri - rr
                        if not 0 <= tap < 5:
                            continue
                        for cc in range(2):
                            for tj in range(5):
                                term = weight[tap * 5 + tj] * xs[cc + tj]
                                acc[rr][cc] = term if acc[rr][cc] is None else acc[rr][cc] + term
                for rr in range(2):
                    for cc in range(2):
                        conv[rr, c0 + cc, :, lanes] = acc[rr][cc]
                return 0

            lax.fori_loop(0, COL // 2, block, 0)

    def mlp(b):
        x = conv[...].reshape(2 * NLON, D)
        mean = jnp.mean(x, axis=1, keepdims=True)
        x = x - mean
        var = jnp.mean(x * x, axis=1, keepdims=True)
        normed = (x * lax.rsqrt(var + 1e-6) * gain[...]).astype(BF)
        h = jnp.dot(normed, up[...], preferred_element_type=F32)
        half = 0.5 * h
        inner = h * (0.7978845608028654 + (0.7978845608028654 * 0.044715) * (h * h))
        hidden = (half + half * jnp.tanh(inner)).astype(BF)
        y = jnp.dot(hidden, down[...], preferred_element_type=F32)
        y = (act[2 + 2 * b : 4 + 2 * b, 2 : 2 + COL].reshape(2 * NLON, D) + y).astype(BF)
        drift = lax.dot_general(y, outw[...], (((1,), (1,)), ((), ())), preferred_element_type=F32)
        for rr in range(2):
            for c in range(COL):
                first = (rr * COL + c) * SEG
                vt[pl.ds(rr * NLON + c, SEG, stride=COL), 0:NCH] = drift[first : first + SEG, :]
        dT = jnp.transpose(vt[...])[0:96, :]
        return drift_scale * dT + noise_scale * nz[b]

    def send_chunk(it, b):
        def one(k, _):
            owner = 3 * k + b

            @pl.when(owner == t)
            def _():
                pltpu.make_async_copy(ob.at[it, b, k], inb.at[it, t], isem.at[it]).start()

            @pl.when(owner != t)
            def _():
                pltpu.make_async_remote_copy(
                    src_ref=ob.at[it, b, k], dst_ref=inb.at[it, t], send_sem=osend.at[it, b], recv_sem=isem.at[it],
                    device_id={"tm": owner}, device_id_type=MESH).start()

            return 0

        lax.fori_loop(0, TILES, one, 0)

    mine_b, mine_k = lax.rem(t, 3), t // 3

    def scan(it):
        retb = (retb0, retb1)[it]
        dst = (st.at[1], stf)[it]

        @pl.when(t < OWNERS)
        def _():
            if it == 0:
                pltpu.make_async_copy(rbuf, rbuf, rootrecv).wait()
            pltpu.make_async_copy(inb.at[it], inb.at[it], isem.at[it]).wait()

            def one(s, acc):
                retb[s] = acc.astype(retb.dtype)
                return acc + inb[it, s].astype(F32)

            lax.fori_loop(0, NT, one, rbuf[...], unroll=8)

            def send(s):
                pltpu.make_async_remote_copy(
                    src_ref=retb.at[s], dst_ref=dst.at[mine_b, mine_k], send_sem=rsend.at[it],
                    recv_sem=stsem.at[it, mine_b], device_id={"tm": s}, device_id_type=MESH).start()

            others(send)
            pltpu.make_async_copy(retb.at[t], dst.at[mine_b, mine_k], stsem.at[it, mine_b]).start()

    def wait_chunk(it, b):
        dst = (st.at[1], stf)[it]
        pltpu.make_async_copy(dst.at[b], dst.at[b], stsem.at[it, b]).wait()

    vt[...] = jnp.zeros(vt.shape, F32)
    for it in range(ITERS):
        for b in (1, 0, 2):
            if it == 1:
                wait_chunk(0, b)
                if b == 0:
                    start_up(1)
                if b == 2:
                    start_down(1)
            embed(from_tiles(st, (it, b)), 2 + 2 * b)
        for b in (1, 0, 2):
            if b == 0:
                @pl.when(l > 0)
                def _():
                    halo_up(it).wait_send()
                    pltpu.make_async_copy(halo.at[it, 0], halo.at[it, 0], hrecv.at[it, 0]).wait()
                    embed(from_tiles(halo, (it, 0)), 0)

                @pl.when(l == 0)
                def _():
                    zero_rows(0)
            if b == 2:
                @pl.when(l < 3)
                def _():
                    halo_down(it).wait_send()
                    pltpu.make_async_copy(halo.at[it, 1], halo.at[it, 1], hrecv.at[it, 1]).wait()
                    embed(from_tiles(halo, (it, 1)), 8)

                @pl.when(l == 3)
                def _():
                    zero_rows(8)
            convolve(b)
            if it == 0 and b == 1:
                meet()
                for r in range(NROW):
                    noise_in(r).wait()
                for bb in range(CHUNKS):
                    nz[bb, 0:NCH, :] = jnp.concatenate([nin[2 * bb], nin[2 * bb + 1]], axis=1)
                    nz[bb, NCH:96, :] = pad
                cup.wait()
                cdown.wait()
            to_tiles(ob, (it, b), mlp(b).astype(BF))
            send_chunk(it, b)
        scan(it)

    for b in (1, 0, 2):
        wait_chunk(1, b)
        value = from_tiles(stf, (b,))[0:NCH, :]
        for rr in range(2):
            tout[2 * b + rr] = value[:, rr * NLON : rr * NLON + NLON]
            state_out(2 * b + rr).start()

    def drain(ref, sem):
        pltpu.make_async_copy(ref, ref, sem).wait()

    @pl.when(t == 0)
    def _():
        drain(rsrc.at[0], rootsend)
        drain(rsrc.at[1], rootsend)
        drain(rsrc.at[2, pl.ds(0, TILES - 1)], rootsend)

    for r in range(NROW):
        state_out(r).wait()

    for it in range(ITERS):
        for b in range(CHUNKS):
            own = jnp.logical_and(mine_b == b, t < OWNERS)

            @pl.when(own)
            def _():
                drain(ob.at[it, b, pl.ds(0, TILES - 1)], osend.at[it, b])

            @pl.when(jnp.logical_not(own))
            def _():
                drain(ob.at[it, b], osend.at[it, b])

        @pl.when(t < OWNERS)
        def _():
            retb = (retb0, retb1)[it]
            drain(retb.at[pl.ds(0, NT - 1)], rsend.at[it])


def shards(traj, noise, step_index, emb, timew, dw, gain, up, down, outw):
    vm = pl.BlockSpec(memory_space=pltpu.VMEM)
    anyspace = pl.BlockSpec(memory_space=pl.ANY)
    dma = pltpu.SemaphoreType.DMA
    result = pl.pallas_call(
        kernel,
        out_shape=jax.ShapeDtypeStruct((NCH, NROW, 1, NLON), F32),
        in_specs=[anyspace, anyspace, pl.BlockSpec(memory_space=pltpu.SMEM), vm, anyspace, vm, vm, anyspace, anyspace, vm],
        out_specs=anyspace,
        scratch_shapes=[
            pltpu.VMEM((D, FF), BF),
            pltpu.VMEM((FF, D), BF),
            pltpu.VMEM((D, D), F32),
            pltpu.VMEM((NROW, NCH, NLON), F32),
            pltpu.VMEM((NROW, NCH, NLON), F32),
            pltpu.VMEM((NROW, NCH, NLON), F32),
            pltpu.VMEM((10, COL + 4, SEG, D), F32),
            pltpu.VMEM((25, 8, D), F32),
            pltpu.VMEM((2, COL, SEG, D), F32),
            pltpu.VMEM((384, 128), F32),
            pltpu.VMEM((96, 384), F32),
            pltpu.VMEM((CHUNKS, 96, 384), F32),
            pltpu.VMEM((8, D), F32),
            pltpu.VMEM((ITERS, CHUNKS, TILES, 16, 128), BF),
            pltpu.VMEM((ITERS, NT, 16, 128), BF),
            pltpu.VMEM((NT, 16, 128), RET[0]),
            pltpu.VMEM((NT, 16, 128), RET[1]),
            pltpu.VMEM((ITERS, CHUNKS, TILES, 16, 128), BF),
            pltpu.VMEM((CHUNKS, TILES, 16, 128), RET[1]),
            pltpu.VMEM((ITERS, 2, TILES, 16, 128), BF),
            pltpu.VMEM((CHUNKS, TILES, 16, 128), F32),
            pltpu.VMEM((16, 128), F32),
            dma((3,)),
            dma((3, NROW)),
            dma((ITERS, CHUNKS)),
            dma((ITERS,)),
            dma((ITERS,)),
            dma((ITERS, CHUNKS)),
            dma((ITERS, 2)),
            dma((ITERS, 2)),
            dma,
            dma,
        ],
        compiler_params=pltpu.CompilerParams(
            collective_id=0, has_side_effects=True, vmem_limit_bytes=56 * 2**20
        ),
    )(
        traj.reshape(NCH, NROW, 1, NLON), noise.reshape(NCH, NROW, 1, NLON), step_index,
        emb, timew, dw.T, gain.reshape(1, D), up, down, outw.T,
    )
    return result.reshape(1, NCH, NROW, NLON)


def solution(mesh):
    in_specs = (
        P("tm", None, "lat", None),
        P("tm", None, "lat", None),
        P("tm"),
        P(), P(), P(), P(), P(), P(), P(),
    )
    out_specs = P("tm", None, "lat", None)
    return jax.shard_map(shards, mesh=mesh, in_specs=in_specs, out_specs=out_specs, check_vma=False)
```

```python
import functools
import math

import jax
import jax.numpy as jnp
from jax import lax
from jax.experimental import pallas as pl
from jax.experimental.pallas import tpu as pltpu
from jax.sharding import PartitionSpec as P

MESH = pl.DeviceIdType.MESH
BF, F32 = jnp.bfloat16, jnp.float32
ITERS = 2
LEVELS = 1000
NCH, NROW, NLON = 83, 6, 192
SEG, COL = 8, 24
NT = 64
CHUNKS, TILES = 3, 18
OWNERS = CHUNKS * TILES
RET = (BF, BF)
D, FF = 512, 1024


def to_tiles(ref, lead, value):
    for lane in range(3):
        for group in range(6):
            ref[lead + (lane * 6 + group,)] = value[group * 16 : group * 16 + 16, lane * 128 : lane * 128 + 128]


def from_tiles(ref, lead):
    lanes = []
    for lane in range(3):
        lanes.append(jnp.concatenate([ref[lead + (lane * 6 + group,)].astype(F32) for group in range(6)], axis=0))
    return jnp.concatenate(lanes, axis=1)


def kernel(
    traj, noise, step, emb, timew_h, taps, gain, up_h, down_h, outw, out,
    up, down, timew, tin, nin, tout, act, wb, conv, vt, dt, nz, condb,
    ob, inb, retb0, retb1, st, stf, halo, rsrc, rbuf,
    wsem, iosem, osend, isem, rsend, stsem, hsend, hrecv, rootsend, rootrecv,
):
    t, l = lax.axis_index("tm"), lax.axis_index("lat")
    y, z, core = t // 16, (t // 2) % 8, t % 2

    def others(do):
        def ring(i, _):
            half = (i + 1) // 2
            dz = jnp.where(i % 2 == 0, 4 + half, 4 - half)
            zz = lax.rem(z + dz, 8) * 2
            for dy in (2, 1, 3, 0):
                yy = lax.rem(y + dy, 4) * 16 + zz
                for dc in (0, 1):
                    do(yy + lax.rem(core + dc, 2))
            return 0

        lax.fori_loop(0, 7, ring, 0)
        for dy in (2, 1, 3, 0):
            for dc in (1, 0):
                if dy or dc:
                    do(lax.rem(y + dy, 4) * 16 + z * 2 + lax.rem(core + dc, 2))

    barrier = pltpu.get_barrier_semaphore()
    for shift in (1, 3):
        pl.semaphore_signal(barrier, inc=1, device_id={"lat": lax.rem(l + shift, 4)}, device_id_type=MESH)
    others(lambda s: pl.semaphore_signal(barrier, inc=1, device_id={"tm": s}, device_id_type=MESH))


    def traj_in(r):
        return pltpu.make_async_copy(traj.at[:, r, 0, :], tin.at[r], iosem.at[0, r])

    def noise_in(r):
        return pltpu.make_async_copy(noise.at[:, r, 0, :], nin.at[r], iosem.at[1, r])

    def state_out(r):
        return pltpu.make_async_copy(tout.at[r], out.at[:, r, 0, :], iosem.at[2, r])

    for r in range(NROW):
        traj_in(r).start()
    ctime = pltpu.make_async_copy(timew_h, timew, wsem.at[2])
    ctime.start()
    for r in range(NROW):
        noise_in(r).start()
    cup = pltpu.make_async_copy(up_h, up, wsem.at[0])
    cdown = pltpu.make_async_copy(down_h, down, wsem.at[1])
    cup.start()
    cdown.start()

    for r in range(NROW):
        traj_in(r).wait()
    pad = jnp.zeros((96 - NCH, 384), F32)
    for b in range(CHUNKS):
        pair = jnp.concatenate([tin[2 * b], tin[2 * b + 1]], axis=1)
        dt[0:NCH, :] = pair
        dt[NCH:96, :] = pad
        whole = dt[0:96, :]
        to_tiles(rsrc.at[b], (), whole)
        to_tiles(st, (0, b), whole.astype(BF))

    stepf = jnp.full((8, 512), step[0].astype(F32), F32)
    level = 2.0 * jnp.exp(stepf * (math.log(0.1) / (LEVELS - 1)))
    j = lax.broadcasted_iota(jnp.int32, (8, 512), 1)
    jj = jnp.where(j < 256, j, j - 256).astype(F32)
    frequency = jnp.exp(jj * (-math.log(100.0) / 256))
    angles = jnp.log(level) * frequency
    features = jnp.where(j < 256, jnp.cos(angles), jnp.sin(angles))
    ctime.wait()
    cond = jnp.dot(features, timew[...], precision=lax.Precision.HIGHEST, preferred_element_type=F32)
    condb[...] = cond * (1.0 / (1.0 + jnp.exp(-cond)))
    drift_scale = 0.125 * level[0:1, 0:384]
    noise_scale = 0.125 * jnp.sqrt(level[0:1, 0:384])

    for k in range(25):
        wb[k] = jnp.broadcast_to(taps[k : k + 1, :], (8, D))

    def halo_up(it):
        return pltpu.make_async_remote_copy(
            src_ref=st.at[it, 0], dst_ref=halo.at[it, 1], send_sem=hsend.at[it, 0], recv_sem=hrecv.at[it, 1],
            device_id={"lat": l - 1}, device_id_type=MESH)

    def halo_down(it):
        return pltpu.make_async_remote_copy(
            src_ref=st.at[it, 2], dst_ref=halo.at[it, 0], send_sem=hsend.at[it, 1], recv_sem=hrecv.at[it, 0],
            device_id={"lat": l + 1}, device_id_type=MESH)

    def start_up(it):
        @pl.when(l > 0)
        def _():
            halo_up(it).start()

    def start_down(it):
        @pl.when(l < 3)
        def _():
            halo_down(it).start()

    def root_copy(k):
        return pltpu.make_async_remote_copy(
            src_ref=rsrc.at[k % 3, k // 3], dst_ref=rbuf, send_sem=rootsend, recv_sem=rootrecv,
            device_id={"tm": k}, device_id_type=MESH)

    def meet():
        pl.semaphore_wait(barrier, NT + 1)
        start_up(0)
        start_down(0)

        @pl.when(t == 0)
        def _():
            pltpu.make_async_copy(rsrc.at[0, 0], rbuf, rootrecv).start()

            def one(k, _):
                root_copy(k).start()
                return 0

            lax.fori_loop(1, OWNERS, one, 0)

    def embed(read, row0):
        vt[:, 0:96] = jnp.transpose(read)

        for rr in range(2):
            cols = [vt[pl.ds(rr * NLON + c, SEG, stride=COL), :] for c in range(COL)]
            lhs = jnp.concatenate(cols, axis=0)[:, 0:NCH].astype(BF)
            value = jnp.dot(lhs, emb[...], preferred_element_type=F32)
            value = value.reshape(COL, SEG, D) + condb[...][None]
            value = value.astype(BF).astype(F32)
            act[row0 + rr, 2 : 2 + COL] = value
            for c in range(2):
                act[row0 + rr, c] = pltpu.roll(value[COL - 2 + c], 1, 0)
                act[row0 + rr, COL + 2 + c] = pltpu.roll(value[c], SEG - 1, 0)

    def zero_rows(row0):
        act[pl.ds(row0, 2)] = jnp.zeros((2, COL + 4, SEG, D), F32)

    def convolve(b):
        for g in range(4):
            lanes = slice(g * 128, g * 128 + 128)
            weight = [wb[k, :, lanes] for k in range(25)]

            def block(cb, _):
                c0 = cb * 2
                acc = [[None] * 2 for _ in range(2)]
                for ri in range(6):
                    xs = [act[2 * b + ri, c0 + ci, :, lanes] for ci in range(6)]
                    for rr in range(2):
                        tap = ri - rr
                        if not 0 <= tap < 5:
                            continue
                        for cc in range(2):
                            for tj in range(5):
                                term = weight[tap * 5 + tj] * xs[cc + tj]
                                acc[rr][cc] = term if acc[rr][cc] is None else acc[rr][cc] + term
                for rr in range(2):
                    for cc in range(2):
                        conv[rr, c0 + cc, :, lanes] = acc[rr][cc]
                return 0

            lax.fori_loop(0, COL // 2, block, 0)

    def mlp(b):
        x = conv[...].reshape(2 * NLON, D)
        mean = jnp.mean(x, axis=1, keepdims=True)
        x = x - mean
        var = jnp.mean(x * x, axis=1, keepdims=True)
        normed = (x * lax.rsqrt(var + 1e-6) * gain[...]).astype(BF)
        h = jnp.dot(normed, up[...], preferred_element_type=F32)
        half = 0.5 * h
        inner = h * (0.7978845608028654 + (0.7978845608028654 * 0.044715) * (h * h))
        hidden = (half + half * jnp.tanh(inner)).astype(BF)
        y = jnp.dot(hidden, down[...], preferred_element_type=F32)
        y = (act[2 + 2 * b : 4 + 2 * b, 2 : 2 + COL].reshape(2 * NLON, D) + y).astype(BF)
        drift = lax.dot_general(y, outw[...], (((1,), (1,)), ((), ())), preferred_element_type=F32)
        for rr in range(2):
            for c in range(COL):
                first = (rr * COL + c) * SEG
                vt[pl.ds(rr * NLON + c, SEG, stride=COL), 0:NCH] = drift[first : first + SEG, :]
        dT = jnp.transpose(vt[...])[0:96, :]
        return drift_scale * dT + noise_scale * nz[b]

    def send_chunk(it, b):
        def one(i, _):
            k = lax.rem(i + t, TILES)
            owner = 3 * k + b

            @pl.when(owner == t)
            def _():
                pltpu.make_async_copy(ob.at[it, b, k], inb.at[it, t], isem.at[it]).start()

            @pl.when(owner != t)
            def _():
                pltpu.make_async_remote_copy(
                    src_ref=ob.at[it, b, k], dst_ref=inb.at[it, t], send_sem=osend.at[it, b], recv_sem=isem.at[it],
                    device_id={"tm": owner}, device_id_type=MESH).start()

            return 0

        lax.fori_loop(0, TILES, one, 0)

    mine_b, mine_k = lax.rem(t, 3), t // 3

    def scan(it):
        retb = (retb0, retb1)[it]
        dst = (st.at[1], stf)[it]

        @pl.when(t < OWNERS)
        def _():
            if it == 0:
                pltpu.make_async_copy(rbuf, rbuf, rootrecv).wait()
            pltpu.make_async_copy(inb.at[it], inb.at[it], isem.at[it]).wait()

            def one(s, acc):
                retb[s] = acc.astype(retb.dtype)
                return acc + inb[it, s].astype(F32)

            lax.fori_loop(0, NT, one, rbuf[...], unroll=8)

            def send(s):
                pltpu.make_async_remote_copy(
                    src_ref=retb.at[s], dst_ref=dst.at[mine_b, mine_k], send_sem=rsend.at[it],
                    recv_sem=stsem.at[it, mine_b], device_id={"tm": s}, device_id_type=MESH).start()

            others(send)
            pltpu.make_async_copy(retb.at[t], dst.at[mine_b, mine_k], stsem.at[it, mine_b]).start()

    def wait_chunk(it, b):
        dst = (st.at[1], stf)[it]
        pltpu.make_async_copy(dst.at[b], dst.at[b], stsem.at[it, b]).wait()

    vt[...] = jnp.zeros(vt.shape, F32)
    for it in range(ITERS):
        for b in (1, 0, 2):
            if it == 1:
                wait_chunk(0, b)
                if b == 0:
                    start_up(1)
                if b == 2:
                    start_down(1)
            embed(from_tiles(st, (it, b)), 2 + 2 * b)
        for b in (1, 0, 2):
            if b == 0:
                @pl.when(l > 0)
                def _():
                    halo_up(it).wait_send()
                    pltpu.make_async_copy(halo.at[it, 0], halo.at[it, 0], hrecv.at[it, 0]).wait()
                    embed(from_tiles(halo, (it, 0)), 0)

                @pl.when(l == 0)
                def _():
                    zero_rows(0)
            if b == 2:
                @pl.when(l < 3)
                def _():
                    halo_down(it).wait_send()
                    pltpu.make_async_copy(halo.at[it, 1], halo.at[it, 1], hrecv.at[it, 1]).wait()
                    embed(from_tiles(halo, (it, 1)), 8)

                @pl.when(l == 3)
                def _():
                    zero_rows(8)
            convolve(b)
            if it == 0 and b == 1:
                meet()
                for r in range(NROW):
                    noise_in(r).wait()
                for bb in range(CHUNKS):
                    nz[bb, 0:NCH, :] = jnp.concatenate([nin[2 * bb], nin[2 * bb + 1]], axis=1)
                    nz[bb, NCH:96, :] = pad
                cup.wait()
                cdown.wait()
            to_tiles(ob, (it, b), mlp(b).astype(BF))
            send_chunk(it, b)
        scan(it)

    for b in (1, 0, 2):
        wait_chunk(1, b)
        value = from_tiles(stf, (b,))[0:NCH, :]
        for rr in range(2):
            tout[2 * b + rr] = value[:, rr * NLON : rr * NLON + NLON]
            state_out(2 * b + rr).start()

    def drain(ref, sem):
        pltpu.make_async_copy(ref, ref, sem).wait()

    @pl.when(t == 0)
    def _():
        drain(rsrc.at[0], rootsend)
        drain(rsrc.at[1], rootsend)
        drain(rsrc.at[2, pl.ds(0, TILES - 1)], rootsend)

    for r in range(NROW):
        state_out(r).wait()

    for it in range(ITERS):
        for b in range(CHUNKS):
            own = jnp.logical_and(mine_b == b, t < OWNERS)

            @pl.when(own)
            def _():
                drain(ob.at[it, b, pl.ds(0, TILES - 1)], osend.at[it, b])

            @pl.when(jnp.logical_not(own))
            def _():
                drain(ob.at[it, b], osend.at[it, b])

        @pl.when(t < OWNERS)
        def _():
            retb = (retb0, retb1)[it]
            drain(retb.at[pl.ds(0, NT - 1)], rsend.at[it])


def shards(traj, noise, step_index, emb, timew, dw, gain, up, down, outw):
    vm = pl.BlockSpec(memory_space=pltpu.VMEM)
    anyspace = pl.BlockSpec(memory_space=pl.ANY)
    dma = pltpu.SemaphoreType.DMA
    result = pl.pallas_call(
        kernel,
        out_shape=jax.ShapeDtypeStruct((NCH, NROW, 1, NLON), F32),
        in_specs=[anyspace, anyspace, pl.BlockSpec(memory_space=pltpu.SMEM), vm, anyspace, vm, vm, anyspace, anyspace, vm],
        out_specs=anyspace,
        scratch_shapes=[
            pltpu.VMEM((D, FF), BF),
            pltpu.VMEM((FF, D), BF),
            pltpu.VMEM((D, D), F32),
            pltpu.VMEM((NROW, NCH, NLON), F32),
            pltpu.VMEM((NROW, NCH, NLON), F32),
            pltpu.VMEM((NROW, NCH, NLON), F32),
            pltpu.VMEM((10, COL + 4, SEG, D), F32),
            pltpu.VMEM((25, 8, D), F32),
            pltpu.VMEM((2, COL, SEG, D), F32),
            pltpu.VMEM((384, 128), F32),
            pltpu.VMEM((96, 384), F32),
            pltpu.VMEM((CHUNKS, 96, 384), F32),
            pltpu.VMEM((8, D), F32),
            pltpu.VMEM((ITERS, CHUNKS, TILES, 16, 128), BF),
            pltpu.VMEM((ITERS, NT, 16, 128), BF),
            pltpu.VMEM((NT, 16, 128), RET[0]),
            pltpu.VMEM((NT, 16, 128), RET[1]),
            pltpu.VMEM((ITERS, CHUNKS, TILES, 16, 128), BF),
            pltpu.VMEM((CHUNKS, TILES, 16, 128), RET[1]),
            pltpu.VMEM((ITERS, 2, TILES, 16, 128), BF),
            pltpu.VMEM((CHUNKS, TILES, 16, 128), F32),
            pltpu.VMEM((16, 128), F32),
            dma((3,)),
            dma((3, NROW)),
            dma((ITERS, CHUNKS)),
            dma((ITERS,)),
            dma((ITERS,)),
            dma((ITERS, CHUNKS)),
            dma((ITERS, 2)),
            dma((ITERS, 2)),
            dma,
            dma,
        ],
        compiler_params=pltpu.CompilerParams(
            collective_id=0, has_side_effects=True, vmem_limit_bytes=56 * 2**20
        ),
    )(
        traj.reshape(NCH, NROW, 1, NLON), noise.reshape(NCH, NROW, 1, NLON), step_index,
        emb, timew, dw.T, gain.reshape(1, D), up, down, outw.T,
    )
    return result.reshape(1, NCH, NROW, NLON)


def solution(mesh):
    in_specs = (
        P("tm", None, "lat", None),
        P("tm", None, "lat", None),
        P("tm"),
        P(), P(), P(), P(), P(), P(), P(),
    )
    out_specs = P("tm", None, "lat", None)
    return jax.shard_map(shards, mesh=mesh, in_specs=in_specs, out_specs=out_specs, check_vma=False)
```
